512 devices in a mesh: blk: 16 (over y, z_lo), band: 32 (over x, z_hi, core).
Axes of the slice: x: 4, y: 8, z: 8 (z_hi: 4, z_lo: 2; z = z_hi * 2 + z_lo), core: 2. Of those that a mesh axis runs over, the one named last changes fastest.
Arguments:
- waveforms: bfloat16 [32, 1024, 3000], P('band', 'blk'), may hold values from -200 to 200
Outputs:
- cross: bfloat16 [2, 384, 1024, 1024], P(None, 'band', 'blk')
The draws below stay inside these ranges and needn't reach their ends.
All inputs are finite; a program needn't handle non-finite values.
Results may differ from the reference program's by a relative error of at most 0.0072.
Values may be sent and summed in bfloat16 or wider, within the bound.
A program may use at most 64 MiB of HBM per device.

```python
import math
import jax
import jax.numpy as jnp
from jax import lax

L = 3000
BINS = 384
HALF = 64
STATIONS = 1024
SEG = 32


def draw_waveforms(key, part):
    keys = jax.random.split(key, 4)
    shape = (SEG, STATIONS, L)
    noise = jnp.clip(jax.random.normal(keys[0], shape, jnp.float32), -4.0, 4.0)
    scales = jnp.exp(jax.random.uniform(keys[2], (SEG, STATIONS, 1), jnp.float32, math.log(0.3), math.log(10.0)))
    samples = jnp.arange(L, dtype=jnp.int32)
    tones = jnp.zeros(shape, jnp.float32)
    for tone in range(4):
        tone_key = jax.random.fold_in(keys[3], tone)
        bins = jax.random.randint(jax.random.fold_in(tone_key, 1), (SEG, 1, 1), 1, BINS + 1)
        shift = jax.random.uniform(jax.random.fold_in(tone_key, 2), (SEG, STATIONS, 1), jnp.float32, -math.pi, math.pi)
        amps = jnp.exp(jax.random.uniform(jax.random.fold_in(tone_key, 3), (SEG, STATIONS, 1), jnp.float32, math.log(0.04), math.log(0.15)))
        phase = (bins * samples[None, None, :] % L).astype(jnp.float32) * (2.0 * math.pi / L)
        tones = tones + amps * jnp.sin(phase + shift)
    values = jnp.clip(scales * (noise + tones), -200.0, 200.0)
    return values.astype(jnp.bfloat16)


def setup_inputs(seed: int = 0) -> dict:
    key_list = jax.random.split(jax.random.key(seed), 2)
    return {
        "waveforms": draw_waveforms(jax.random.fold_in(key_list[1], 71), 0),
    }


def make_table():
    samples = jnp.arange(L, dtype=jnp.int32)
    freqs = jnp.arange(1, BINS + 1, dtype=jnp.int32)
    phase = (freqs[:, None] * samples[None, :] % L).astype(jnp.float32) * (2.0 * math.pi / L)
    return jnp.concatenate([jnp.cos(phase), -jnp.sin(phase)], axis=0).astype(jnp.bfloat16)

def make_band():
    freqs = jnp.arange(BINS, dtype=jnp.int32)
    near = (jnp.abs(freqs[:, None] - freqs[None, :]) <= HALF).astype(jnp.float32)
    return near / lax.optimization_barrier(jnp.sum(near, axis=1, keepdims=True))

def reference(waveforms):
    table = make_table()
    band = make_band()

    def whiten(segment):
        values = segment.astype(jnp.float32)
        centred = values - lax.optimization_barrier(jnp.mean(values, axis=1, keepdims=True))
        normed = (centred * lax.rsqrt(lax.optimization_barrier(jnp.mean(centred * centred, axis=1, keepdims=True)) + 1e-05)).astype(jnp.bfloat16)
        raw = lax.dot_general(table, normed, (((1,), (1,)), ((), ())), preferred_element_type=jnp.float32)
        raw = raw.reshape(2, BINS, raw.shape[1])
        power = raw[0] * raw[0] + raw[1] * raw[1]
        smooth = jnp.dot(band, power, precision=lax.Precision.HIGHEST)
        return (raw * lax.rsqrt(smooth + 1e-05)[None]).astype(jnp.bfloat16)
    spectra = lax.map(whiten, waveforms)
    by_bin = jnp.transpose(spectra, (2, 1, 0, 3))
    scale = 1.0 / SEG

    def stack_bin(pair):
        real_part, imag_part = (pair[0], pair[1])
        real_sum = jnp.dot(real_part.T, real_part, preferred_element_type=jnp.float32) + jnp.dot(imag_part.T, imag_part, preferred_element_type=jnp.float32)
        imag_sum = jnp.dot(imag_part.T, real_part, preferred_element_type=jnp.float32) - jnp.dot(real_part.T, imag_part, preferred_element_type=jnp.float32)
        return (jnp.stack([real_sum, imag_sum]) * scale).astype(jnp.bfloat16)
    stacked = lax.map(stack_bin, by_bin)
    return jnp.transpose(stacked, (1, 0, 2, 3))
```

```python
import functools
import math

import jax
import jax.numpy as jnp
import numpy as np
import ml_dtypes
from jax import lax
from jax.experimental import pallas as pl
from jax.experimental.pallas import tpu as pltpu
from jax.sharding import PartitionSpec as P

L = 3000
BINS = 384
HALF = 64
QUARTER = 750
QPAD = 768
SPAD = 3072
PER = 12
ROWS = 16
NSEG = 32
NY = 8
MESH = pl.DeviceIdType.MESH
DCH, ECH = 0, 1
HALFBINS = PER // 2


def make_table():
    freqs = np.arange(1, BINS + 1, dtype=np.int64)
    samples = np.arange(QUARTER, dtype=np.int64)
    phase = ((freqs[:, None] * samples[None, :]) % L).astype(np.float64) * (2.0 * math.pi / L)
    table = np.zeros((2 * BINS, QPAD), np.float32)
    table[:BINS, :QUARTER] = np.cos(phase)
    table[BINS:, :QUARTER] = -np.sin(phase)
    return table.astype(ml_dtypes.bfloat16)


def ring_goes(step, direction, kind):
    if step <= 3:
        return True
    if step > 4:
        return False
    return (kind == 1) if direction else (kind != 1)


KINDS = ((0, ECH), (0, DCH), (1, DCH))


def whiten(xv, tv, n32, x4, zs, spec, send, table_ready):
    for block in range(4):
        rows = pl.ds(16 * block, 16)
        values = xv[rows, :].astype(jnp.float32)
        centred = values - jnp.sum(values, axis=1, keepdims=True) * (1.0 / L)
        var = jnp.sum(centred * centred, axis=1, keepdims=True) * (1.0 / L)
        n32[rows, SPAD - 128 :] = jnp.zeros((16, 128), jnp.float32)
        n32[rows, :L] = centred * lax.rsqrt(var + 1e-05)
        x4[rows, :] = n32[rows, :QPAD].astype(jnp.bfloat16)
        for q in range(1, 4):
            start = QUARTER * q // 128 * 128
            off = QUARTER * q - start
            window = n32[rows, start : start + 896]
            window = pltpu.roll(window, 896 - off, 1)
            x4[pl.ds(64 * q + 16 * block, 16), :] = window[:, :QPAD].astype(jnp.bfloat16)

    table_ready()
    zs[...] = lax.dot_general(
        tv[...], x4[...], (((1,), (1,)), ((), ())), preferred_element_type=jnp.float32
    )

    shape = (96, 128)
    row = lax.broadcasted_iota(jnp.int32, shape, 0)
    lane = lax.broadcasted_iota(jnp.int32, shape, 1)
    low = lane < 64
    phase = row % 4
    even = phase % 2 == 1
    sigma = jnp.where(even, 1.0, -1.0)
    kappa = jnp.where(
        phase == 1, -1.0, jnp.where(phase == 3, 1.0, jnp.where((phase == 0) == low, 1.0, -1.0))
    )
    for part in range(4):
        rows = slice(96 * part, 96 * part + 96)
        irows = slice(BINS + 96 * part, BINS + 96 * part + 96)
        a_sum = zs[rows, :128] + sigma * zs[rows, 128:]
        b_sum = zs[irows, :128] + sigma * zs[irows, 128:]
        a_roll = pltpu.roll(a_sum, 64, 1)
        b_roll = pltpu.roll(b_sum, 64, 1)
        first = jnp.where(low, a_sum, b_roll)
        other = jnp.where(
            even, jnp.where(low, a_roll, b_sum), jnp.where(low, b_roll, a_sum)
        )
        raw = first + kappa * other
        spec[rows, :] = raw
        square = raw * raw
        power = square + pltpu.roll(square, 64, 1)
        high = power.astype(jnp.bfloat16).astype(jnp.float32)
        n32[rows, :128] = jnp.where(low, high, power - high)

    frow = lax.broadcasted_iota(jnp.int32, (BINS, BINS), 0)
    gcol = lax.broadcasted_iota(jnp.int32, (BINS, BINS), 1)
    near = jnp.where(jnp.abs(frow - gcol) <= HALF, 1.0, 0.0).astype(jnp.bfloat16)
    total = jnp.dot(
        near, n32[:BINS, :128].astype(jnp.bfloat16), preferred_element_type=jnp.float32
    )
    frow = lax.broadcasted_iota(jnp.int32, (BINS, 128), 0)
    count = jnp.minimum(frow + HALF, BINS - 1) - jnp.maximum(frow - HALF, 0) + 1
    smooth = (total + pltpu.roll(total, 64, 1)) / count.astype(jnp.float32)
    spec[:BINS, :] = spec[:BINS, :] * lax.rsqrt(smooth + 1e-05)
    spec[BINS:, :] = jnp.zeros((8, 128), jnp.float32)
    for dev in range(NSEG):
        send[dev] = spec[pl.ds(PER * dev, ROWS), :].astype(jnp.bfloat16)


def kernel(
    x_hbm, t_hbm, o_ref,
    xv, tv, n32, x4, zs, spec, send, recv, r32, gath, wt,
    in_sem, a_send, a_recv, y_send, y_recv, z_send, z_recv,
):
    blk = lax.axis_index("blk")
    band = lax.axis_index("band")
    yy = blk // 2
    zz = lax.rem(blk, 2)
    right = lax.rem(yy + 1, NY) * 2 + zz
    left = lax.rem(yy + NY - 1, NY) * 2 + zz
    partner = yy * 2 + 1 - zz

    x_copy = pltpu.make_async_copy(x_hbm.at[0], xv, in_sem.at[0])
    t_copy = pltpu.make_async_copy(t_hbm, tv, in_sem.at[1])
    x_copy.start()
    t_copy.start()

    barrier = pltpu.get_barrier_semaphore()
    for other in (left, right, partner):
        pl.semaphore_signal(barrier, inc=1, device_id={"blk": other, "band": band}, device_id_type=MESH)

    def greet(k, carry):
        pl.semaphore_signal(
            barrier,
            inc=1,
            device_id={"blk": blk, "band": lax.rem(band + k, NSEG)},
            device_id_type=MESH,
        )
        return carry

    lax.fori_loop(1, NSEG, greet, 0)

    x_copy.wait()
    whiten(xv, tv, n32, x4, zs, spec, send, t_copy.wait)

    pl.semaphore_wait(barrier, 3 + NSEG - 1)

    def scatter(k, carry):
        to = lax.rem(band + k, NSEG)
        pltpu.make_async_remote_copy(
            src_ref=send.at[to],
            dst_ref=recv.at[k],
            send_sem=a_send,
            recv_sem=a_recv,
            device_id={"blk": blk, "band": to},
            device_id_type=MESH,
        ).start()
        return carry

    lax.fori_loop(1, NSEG, scatter, 0)
    recv[0] = send[band]
    rest = pl.ds(1, NSEG - 1)
    pltpu.make_async_copy(recv.at[rest], recv.at[rest], a_recv).wait()

    for seg in range(NSEG):
        r32[pl.ds(ROWS * seg, ROWS), :] = recv[seg].astype(jnp.float32)
    for f in range(PER):
        gath[0, 0, f] = r32[pl.ds(f, NSEG, stride=ROWS), :].astype(jnp.bfloat16)

    def bins(half):
        return pl.ds(HALFBINS * half, HALFBINS)

    started = []

    def z_copy(slot, half):
        return pltpu.make_async_remote_copy(
            src_ref=gath.at[0, slot, bins(half)],
            dst_ref=gath.at[1, slot, bins(half)],
            send_sem=z_send.at[slot, half],
            recv_sem=z_recv.at[slot, half],
            device_id={"blk": partner, "band": band},
            device_id_type=MESH,
        )

    def y_copy(step, direction, kind):
        plane, half = KINDS[kind]
        source = (step - 1) if direction == 0 else (NY - step + 1) % NY
        target = step if direction == 0 else NY - step
        return pltpu.make_async_remote_copy(
            src_ref=gath.at[plane, source, bins(half)],
            dst_ref=gath.at[plane, target, bins(half)],
            send_sem=y_send.at[step - 1, direction, kind],
            recv_sem=y_recv.at[step - 1, direction, kind],
            device_id={"blk": (right, left)[direction], "band": band},
            device_id_type=MESH,
        )

    def start(copy):
        copy.start()
        started.append(copy)

    def stack(slots, half):
        lanes = [
            pl.ds(pl.multiple_of(lax.rem(yy + NY - slot, NY) * 128, 128), 128) for slot in slots
        ]

        def one(f, carry):
            for slot, columns in zip(slots, lanes):
                g0 = gath[zz, slot, f]
                g1 = gath[1 - zz, slot, f]
                top = jnp.concatenate([g0[:, :64], g1[:, :64]], axis=1)
                bottom = jnp.concatenate([g0[:, 64:], g1[:, 64:]], axis=1)
                both = jnp.concatenate([top, bottom], axis=0)
                out = jnp.dot(wt[f], both, preferred_element_type=jnp.float32)
                out = out.astype(jnp.bfloat16)
                o_ref[0, f, :, columns] = out[:64]
                o_ref[1, f, :, columns] = out[64:]
            return carry

        lax.fori_loop(HALFBINS * half, HALFBINS * half + HALFBINS, one, 0)

    start(z_copy(0, DCH))
    for kind in (0, 1):
        for direction in (0, 1):
            start(y_copy(1, direction, kind))
    start(z_copy(0, ECH))

    wlow = lax.broadcasted_iota(jnp.int32, (NSEG, 128), 1) < 64
    for f in range(PER):
        own = r32[pl.ds(f, NSEG, stride=ROWS), :] * (1.0 / NSEG)
        turned = pltpu.roll(own, 64, 1)
        turned = jnp.where(wlow, turned, -turned)
        wt[f] = jnp.transpose(jnp.concatenate([own, turned], axis=0)).astype(jnp.bfloat16)

    z_copy(0, DCH).wait_recv()
    for direction in (0, 1):
        start(y_copy(1, direction, 2))
    stack((0,), DCH)

    previous = (0,)
    for step in range(1, 5):
        for kind, (plane, half) in enumerate(KINDS):
            for direction in (0, 1):
                if not ring_goes(step, direction, kind):
                    continue
                slot = step if direction == 0 else NY - step
                y_copy(step, direction, kind).wait_recv()
                if ring_goes(step + 1, direction, kind):
                    start(y_copy(step + 1, direction, kind))
                if plane == 0 and half == ECH:
                    start(z_copy(slot, ECH))
        for slot in previous:
            z_copy(slot, ECH).wait_recv()
        stack(previous, ECH)
        slots = (step, NY - step) if step < 4 else (4,)
        stack(slots, DCH)
        previous = slots
    for slot in previous:
        z_copy(slot, ECH).wait_recv()
    stack(previous, ECH)

    for copy in started:
        copy.wait_send()
    pltpu.make_async_copy(send.at[rest], send.at[rest], a_send).wait()


def shards(waveforms):
    table = jnp.asarray(make_table())
    bf16, f32 = jnp.bfloat16, jnp.float32
    return pl.pallas_call(
        kernel,
        out_shape=jax.ShapeDtypeStruct((2, PER, 64, 1024), bf16),
        in_specs=[pl.BlockSpec(memory_space=pl.ANY)] * 2,
        out_specs=pl.BlockSpec(memory_space=pltpu.VMEM),
        scratch_shapes=[
            pltpu.VMEM((64, L), bf16),
            pltpu.VMEM((2 * BINS, QPAD), bf16),
            pltpu.VMEM((BINS, SPAD), f32),
            pltpu.VMEM((256, QPAD), bf16),
            pltpu.VMEM((2 * BINS, 256), f32),
            pltpu.VMEM((BINS + 8, 128), f32),
            pltpu.VMEM((NSEG, ROWS, 128), bf16),
            pltpu.VMEM((NSEG, ROWS, 128), bf16),
            pltpu.VMEM((NSEG * ROWS, 128), f32),
            pltpu.VMEM((2, NY, PER, NSEG, 128), bf16),
            pltpu.VMEM((PER, 128, 64), bf16),
            pltpu.SemaphoreType.DMA((2,)),
            pltpu.SemaphoreType.DMA,
            pltpu.SemaphoreType.DMA,
            pltpu.SemaphoreType.DMA((4, 2, 3)),
            pltpu.SemaphoreType.DMA((4, 2, 3)),
            pltpu.SemaphoreType.DMA((NY, 2)),
            pltpu.SemaphoreType.DMA((NY, 2)),
        ],
        compiler_params=pltpu.CompilerParams(
            collective_id=0, has_side_effects=True, vmem_limit_bytes=40 * 1024 * 1024
        ),
        cost_estimate=pl.CostEstimate(
            flops=600_000_000, bytes_accessed=6_000_000, transcendentals=50_000
        ),
    )(waveforms, table)


def solution(mesh):
    return jax.shard_map(
        shards,
        mesh=mesh,
        in_specs=(P("band", "blk", None),),
        out_specs=P(None, "band", "blk", None),
        check_vma=False,
    )
```

```python
import functools
import math

import jax
import jax.numpy as jnp
import numpy as np
import ml_dtypes
from jax import lax
from jax.experimental import pallas as pl
from jax.experimental.pallas import tpu as pltpu
from jax.sharding import PartitionSpec as P

L = 3000
BINS = 384
HALF = 64
QUARTER = 750
QPAD = 768
SPAD = 3072
PER = 12
ROWS = 16
NSEG = 32
NY = 8
MESH = pl.DeviceIdType.MESH
NHI = 16
UNROLL = 6
TABLES = 16


def make_table():
    freqs = np.arange(1, BINS + 1, dtype=np.int64)
    samples = np.arange(QUARTER, dtype=np.int64)
    phase = ((freqs[:, None] * samples[None, :]) % L).astype(np.float64) * (2.0 * math.pi / L)
    table = np.zeros((TABLES, 2 * BINS, QPAD), ml_dtypes.bfloat16)
    table[0, :BINS, :QUARTER] = np.cos(phase).astype(np.float32).astype(ml_dtypes.bfloat16)
    table[0, BINS:, :QUARTER] = (-np.sin(phase)).astype(np.float32).astype(ml_dtypes.bfloat16)
    return table


KINDS = ((0, 0), (0, 1), (1, 1))


def ring_goes(step, direction, kind):
    if step <= 3:
        return True
    return step == 4 and (kind == 2 or kind == direction)


def whiten(xv, tv, n32, x4, zs, spec, send, table_ready):
    for block in range(4):
        rows = pl.ds(16 * block, 16)
        values = xv[rows, :].astype(jnp.float32)
        centred = values - jnp.sum(values, axis=1, keepdims=True) * (1.0 / L)
        var = jnp.sum(centred * centred, axis=1, keepdims=True) * (1.0 / L)
        n32[rows, SPAD - 128 :] = jnp.zeros((16, 128), jnp.float32)
        n32[rows, :L] = centred * lax.rsqrt(var + 1e-05)
        x4[rows, :] = n32[rows, :QPAD].astype(jnp.bfloat16)
        for q in range(1, 4):
            start = QUARTER * q // 128 * 128
            off = QUARTER * q - start
            window = n32[rows, start : start + 896]
            window = pltpu.roll(window, 896 - off, 1)
            x4[pl.ds(64 * q + 16 * block, 16), :] = window[:, :QPAD].astype(jnp.bfloat16)

    table_ready()
    zs[...] = lax.dot_general(
        tv[...], x4[...], (((1,), (1,)), ((), ())), preferred_element_type=jnp.float32
    )

    shape = (96, 128)
    row = lax.broadcasted_iota(jnp.int32, shape, 0)
    lane = lax.broadcasted_iota(jnp.int32, shape, 1)
    low = lane < 64
    phase = row % 4
    even = phase % 2 == 1
    sigma = jnp.where(even, 1.0, -1.0)
    kappa = jnp.where(
        phase == 1, -1.0, jnp.where(phase == 3, 1.0, jnp.where((phase == 0) == low, 1.0, -1.0))
    )
    for part in range(4):
        rows = slice(96 * part, 96 * part + 96)
        irows = slice(BINS + 96 * part, BINS + 96 * part + 96)
        a_sum = zs[rows, :128] + sigma * zs[rows, 128:]
        b_sum = zs[irows, :128] + sigma * zs[irows, 128:]
        a_roll = pltpu.roll(a_sum, 64, 1)
        b_roll = pltpu.roll(b_sum, 64, 1)
        first = jnp.where(low, a_sum, b_roll)
        other = jnp.where(
            even, jnp.where(low, a_roll, b_sum), jnp.where(low, b_roll, a_sum)
        )
        raw = first + kappa * other
        spec[rows, :] = raw
        square = raw * raw
        power = square + pltpu.roll(square, 64, 1)
        high = power.astype(jnp.bfloat16).astype(jnp.float32)
        n32[rows, :128] = jnp.where(low, high, power - high)

    frow = lax.broadcasted_iota(jnp.int32, (BINS, BINS), 0)
    gcol = lax.broadcasted_iota(jnp.int32, (BINS, BINS), 1)
    near = jnp.where(jnp.abs(frow - gcol) <= HALF, 1.0, 0.0).astype(jnp.bfloat16)
    total = jnp.dot(
        near, n32[:BINS, :128].astype(jnp.bfloat16), preferred_element_type=jnp.float32
    )
    frow = lax.broadcasted_iota(jnp.int32, (BINS, 128), 0)
    count = jnp.minimum(frow + HALF, BINS - 1) - jnp.maximum(frow - HALF, 0) + 1
    smooth = (total + pltpu.roll(total, 64, 1)) / count.astype(jnp.float32)
    spec[:BINS, :] = spec[:BINS, :] * lax.rsqrt(smooth + 1e-05)
    spec[BINS:, :] = jnp.zeros((8, 128), jnp.float32)
    for dev in range(NSEG):
        send[dev] = spec[pl.ds(PER * dev, ROWS), :].astype(jnp.bfloat16)


def kernel(
    xv, t_hbm, o_ref,
    tv, n32, x4, zs, spec, send, recv, r32, gath, wt,
    in_sem, a_send, a_recv, s_send, s_recv, y_send, y_recv, z_send, z_recv,
):
    blk = lax.axis_index("blk")
    band = lax.axis_index("band")
    yy = blk // 2
    zz = lax.rem(blk, 2)
    hi = band // 2
    core = lax.rem(band, 2)
    right = lax.rem(yy + 1, NY) * 2 + zz
    left = lax.rem(yy + NY - 1, NY) * 2 + zz
    partner = yy * 2 + 1 - zz
    sibling = hi * 2 + 1 - core

    barrier = pltpu.get_barrier_semaphore()

    def greet(k, carry):
        pl.semaphore_signal(
            barrier,
            inc=1,
            device_id={"blk": blk, "band": lax.rem(band + k, NSEG)},
            device_id_type=MESH,
        )
        return carry

    t_copy = pltpu.make_async_copy(t_hbm.at[0], tv, in_sem)
    t_copy.start()
    for other in (left, right, partner):
        pl.semaphore_signal(
            barrier, inc=1, device_id={"blk": other, "band": band}, device_id_type=MESH
        )
    lax.fori_loop(1, NSEG, greet, 0)

    whiten(xv.at[0], tv, n32, x4, zs, spec, send, t_copy.wait)

    pl.semaphore_wait(barrier, 3 + NSEG - 1)

    def scatter(m, carry):
        for c in (0, 1):
            to = lax.rem(hi + m, NHI) * 2 + c
            pltpu.make_async_remote_copy(
                src_ref=send.at[to],
                dst_ref=recv.at[core, m],
                send_sem=a_send,
                recv_sem=a_recv.at[core],
                device_id={"blk": blk, "band": to},
                device_id_type=MESH,
            ).start()
        return carry

    lax.fori_loop(1, NHI, scatter, 0)
    to_sibling = pltpu.make_async_remote_copy(
        src_ref=send.at[sibling],
        dst_ref=recv.at[core, 0],
        send_sem=s_send,
        recv_sem=s_recv,
        device_id={"blk": blk, "band": sibling},
        device_id_type=MESH,
    )
    to_sibling.start()
    recv[core, 0] = send[band]
    others = pl.ds(1, NHI - 1)

    def collect(c):
        pltpu.make_async_copy(recv.at[c, others], recv.at[c, others], a_recv.at[c]).wait()
        pl.when(core != c)(to_sibling.wait_recv)
        for m in range(NHI):
            r32[c, pl.ds(ROWS * m, ROWS), :] = recv[c, m].astype(jnp.float32)
        for f in range(PER):
            gath[0, 0, c, f] = r32[c, pl.ds(f, NHI, stride=ROWS), :].astype(jnp.bfloat16)

    started = []

    def z_copy(slot, c):
        return pltpu.make_async_remote_copy(
            src_ref=gath.at[0, slot, c],
            dst_ref=gath.at[1, slot, c],
            send_sem=z_send.at[slot, c],
            recv_sem=z_recv.at[slot, c],
            device_id={"blk": partner, "band": band},
            device_id_type=MESH,
        )

    def y_copy(step, direction, kind):
        plane, c = KINDS[kind]
        source = (step - 1) if direction == 0 else (NY - step + 1) % NY
        target = step if direction == 0 else NY - step
        part = pl.ds(PER // 2 * direction, PER // 2) if (step, kind) == (4, 2) else pl.ds(0, PER)
        return pltpu.make_async_remote_copy(
            src_ref=gath.at[plane, source, c, part],
            dst_ref=gath.at[plane, target, c, part],
            send_sem=y_send.at[step - 1, direction, kind],
            recv_sem=y_recv.at[step - 1, direction, kind],
            device_id={"blk": (right, left)[direction], "band": band},
            device_id_type=MESH,
        )

    def start(copy):
        copy.start()
        started.append(copy)

    def stack(slots):
        columns = [
            pl.ds(pl.multiple_of(lax.rem(yy + NY - slot, NY) * 128, 128), 128) for slot in slots
        ]

        def pair(slot, f):
            g0 = jnp.concatenate([gath[zz, slot, 0, f], gath[zz, slot, 1, f]], axis=0)
            g1 = jnp.concatenate([gath[1 - zz, slot, 0, f], gath[1 - zz, slot, 1, f]], axis=0)
            top = jnp.concatenate([g0[:, :64], g1[:, :64]], axis=1)
            bottom = jnp.concatenate([g0[:, 64:], g1[:, 64:]], axis=1)
            return jnp.concatenate([top, bottom], axis=0)

        def some(i, carry):
            for u in range(UNROLL):
                f = i * UNROLL + u
                both = jnp.concatenate([pair(slot, f) for slot in slots], axis=1)
                out = jnp.dot(wt[f], both, preferred_element_type=jnp.float32)
                out = out.astype(jnp.bfloat16)
                for k, where in enumerate(columns):
                    lanes = slice(128 * k, 128 * k + 128)
                    o_ref[0, f, :, where] = out[:64, lanes]
                    o_ref[1, f, :, where] = out[64:, lanes]
            return carry

        lax.fori_loop(0, PER // UNROLL, some, 0)

    collect(0)
    for direction in (0, 1):
        start(y_copy(1, direction, 0))
    start(z_copy(0, 0))
    collect(1)
    start(z_copy(0, 1))
    for direction in (0, 1):
        start(y_copy(1, direction, 1))

    wlow = lax.broadcasted_iota(jnp.int32, (NSEG, 128), 1) < 64
    for f in range(PER):
        own = jnp.concatenate(
            [r32[c, pl.ds(f, NHI, stride=ROWS), :] for c in (0, 1)], axis=0
        ) * (1.0 / NSEG)
        turned = pltpu.roll(own, 64, 1)
        turned = jnp.where(wlow, turned, -turned)
        wt[f] = jnp.transpose(jnp.concatenate([own, turned], axis=0)).astype(jnp.bfloat16)

    z_copy(0, 1).wait_recv()
    for direction in (0, 1):
        start(y_copy(1, direction, 2))

    previous = (0,)
    for step in range(1, 5):
        for kind in range(3):
            for direction in (0, 1):
                if not ring_goes(step, direction, kind):
                    continue
                slot = step if direction == 0 else NY - step
                y_copy(step, direction, kind).wait_recv()
                if ring_goes(step + 1, direction, kind):
                    start(y_copy(step + 1, direction, kind))
                if kind == 0:
                    start(z_copy(slot, 0))
        for slot in previous:
            z_copy(slot, 0).wait_recv()
        stack(previous)
        previous = (step, NY - step) if step < 4 else (4,)
    z_copy(4, 0).wait_recv()
    stack(previous)

    for copy in started:
        copy.wait_send()
    to_sibling.wait_send()
    for half in (0, 1):
        rest = pl.ds(0, NHI - 1)
        pltpu.make_async_copy(send.at[rest], send.at[rest], a_send).wait()


def shards(waveforms):
    table = jnp.asarray(make_table())
    bf16, f32 = jnp.bfloat16, jnp.float32
    return pl.pallas_call(
        kernel,
        out_shape=jax.ShapeDtypeStruct((2, PER, 64, 1024), bf16),
        in_specs=[
            pl.BlockSpec(memory_space=pltpu.VMEM),
            pl.BlockSpec(memory_space=pl.ANY),
        ],
        out_specs=pl.BlockSpec(memory_space=pltpu.VMEM),
        scratch_shapes=[
            pltpu.VMEM((2 * BINS, QPAD), bf16),
            pltpu.VMEM((BINS, SPAD), f32),
            pltpu.VMEM((256, QPAD), bf16),
            pltpu.VMEM((2 * BINS, 256), f32),
            pltpu.VMEM((BINS + 8, 128), f32),
            pltpu.VMEM((NSEG, ROWS, 128), bf16),
            pltpu.VMEM((2, NHI, ROWS, 128), bf16),
            pltpu.VMEM((2, NHI * ROWS, 128), f32),
            pltpu.VMEM((2, NY, 2, PER, NHI, 128), bf16),
            pltpu.VMEM((PER, 128, 64), bf16),
            pltpu.SemaphoreType.DMA,
            pltpu.SemaphoreType.DMA,
            pltpu.SemaphoreType.DMA((2,)),
            pltpu.SemaphoreType.DMA,
            pltpu.SemaphoreType.DMA,
            pltpu.SemaphoreType.DMA((4, 2, 3)),
            pltpu.SemaphoreType.DMA((4, 2, 3)),
            pltpu.SemaphoreType.DMA((NY, 2)),
            pltpu.SemaphoreType.DMA((NY, 2)),
        ],
        compiler_params=pltpu.CompilerParams(
            collective_id=0, has_side_effects=True, vmem_limit_bytes=44 * 1024 * 1024
        ),
        cost_estimate=pl.CostEstimate(
            flops=600_000_000, bytes_accessed=6_000_000, transcendentals=50_000
        ),
    )(waveforms, table)


def solution(mesh):
    return jax.shard_map(
        shards,
        mesh=mesh,
        in_specs=(P("band", "blk", None),),
        out_specs=P(None, "band", "blk", None),
        check_vma=False,
    )
```

```python
import heapq
import math

import jax
import jax.numpy as jnp
import numpy as np
import ml_dtypes
from jax import lax
from jax.experimental import pallas as pl
from jax.experimental.pallas import tpu as pltpu
from jax.sharding import PartitionSpec as P

L = 3000
BINS = 384
HALF = 64
QUARTER = 750
QPAD = 768
SPAD = 3072
PER = 12
ROWS = 16
NSEG = 32
NY = 8
MESH = pl.DeviceIdType.MESH
NHI = 16
TABLES = 16


def make_table():
    freqs = np.arange(1, BINS + 1, dtype=np.int64)
    samples = np.arange(QUARTER, dtype=np.int64)
    phase = ((freqs[:, None] * samples[None, :]) % L).astype(np.float64) * (2.0 * math.pi / L)
    table = np.zeros((TABLES, 2 * BINS, QPAD), ml_dtypes.bfloat16)
    table[0, :BINS, :QUARTER] = np.cos(phase).astype(np.float32).astype(ml_dtypes.bfloat16)
    table[0, BINS:, :QUARTER] = (-np.sin(phase)).astype(np.float32).astype(ml_dtypes.bfloat16)
    return table


PARTS = 3
PIECES = [(c, p) for c in (0, 1) for p in range(PARTS)]
Y_FIRST = PIECES[:4]
DIAGONAL = True
SKIP = True
DY = (1, -1, 2, -2)
LATENCY, HOP, LATE, GAP = 2.6, 0.55, 1.0, 0.1


def make_plan():
    unit, cost = 1.07 / PARTS, 0.06
    last = {}
    for plane in (0, 1):
        for piece in PIECES:
            if plane == 0 or piece not in Y_FIRST:
                last[plane, *piece] = (1, -1)[len(last) % 2]
    free = {1: 0.0, -1: 0.0, 0: 0.0}
    arrivals, plan = [], []
    now = 0.0

    def start(plane, slot, piece, dy, dz):
        nonlocal now
        now += cost
        sign = (dy > 0) - (dy < 0)
        links = ([sign] if dy else []) + ([0] if dz else [])
        begin = max([free[k] for k in links] + [now])
        for k in links:
            free[k] = max(free[k], begin) + unit * (abs(dy) if k else 1)
        copy = (plane, slot, *piece, dy, dz)
        arrival = begin + unit + LATENCY + HOP * (abs(dy) + dz - 1)
        heapq.heappush(arrivals, (arrival, len(plan), copy))
        plan.append(("start", copy))

    for core in (0, 1):
        mine = [piece for piece in PIECES if piece[0] == core]
        if core == 1:
            plan.append(("second",))
            now = max(now, LATE)
        for piece in mine:
            if piece not in Y_FIRST:
                start(0, 0, piece, 0, 1)
        for piece in mine:
            for sign in (1, -1):
                start(0, 0, piece, sign, 0)
            if piece not in Y_FIRST and DIAGONAL:
                for sign in (1, -1):
                    start(0, 0, piece, sign, 1)
        for piece in mine:
            if piece in Y_FIRST:
                start(0, 0, piece, 0, 1)
    missing = {(slot, p): 4 if slot else 2 for slot in range(NY) for p in range(PARTS)}
    groups = [(0,), (1, 7), (2, 6), (3, 5), (4,)]
    ready = []
    while arrivals:
        while ready and arrivals[0][0] - now > GAP:
            plan.append(ready.pop(0))
            now += GAP
        when, _, copy = heapq.heappop(arrivals)
        now = max(now, when) + cost
        plan.append(("wait", copy))
        plane, slot, core, part, dy, dz = copy
        piece = (core, part)
        plane, slot = (plane + dz) % 2, (slot + dy) % NY
        sign = (dy > 0) - (dy < 0)
        first_cross = plane == 1 and piece not in Y_FIRST
        if dy == 0:
            if slot == 0 and first_cross and not DIAGONAL:
                for sign in (1, -1):
                    start(1, 0, piece, sign, 0)
        elif plane == 0 or first_cross:
            distance = min(slot, NY - slot)
            if distance < 3:
                start(plane, slot, piece, sign, 0)
            if last[plane, core, part] == sign and distance == (2 if SKIP else 3):
                start(plane, slot, piece, (2 if SKIP else 1) * sign, 0)
            if plane == 0 and piece in Y_FIRST:
                start(0, slot, piece, 0, 1)
        missing[slot, part] -= 1
        for group in groups:
            if slot in group and not any(missing[k, part] for k in group):
                ready.append(("stack", group, part))
    plan.extend(ready)
    assert not any(missing.values())
    return plan


def whiten(xv, tv, n32, x4, zs, spec, send, table_ready):
    for block in range(4):
        rows = pl.ds(16 * block, 16)
        values = xv[rows, :].astype(jnp.float32)
        centred = values - jnp.sum(values, axis=1, keepdims=True) * (1.0 / L)
        var = jnp.sum(centred * centred, axis=1, keepdims=True) * (1.0 / L)
        n32[rows, SPAD - 128 :] = jnp.zeros((16, 128), jnp.float32)
        n32[rows, :L] = centred * lax.rsqrt(var + 1e-05)
        x4[rows, :] = n32[rows, :QPAD].astype(jnp.bfloat16)
        for q in range(1, 4):
            start = QUARTER * q // 128 * 128
            off = QUARTER * q - start
            window = n32[rows, start : start + 896]
            window = pltpu.roll(window, 896 - off, 1)
            x4[pl.ds(64 * q + 16 * block, 16), :] = window[:, :QPAD].astype(jnp.bfloat16)

    table_ready()
    zs[...] = lax.dot_general(
        tv[...], x4[...], (((1,), (1,)), ((), ())), preferred_element_type=jnp.float32
    )

    shape = (96, 128)
    row = lax.broadcasted_iota(jnp.int32, shape, 0)
    lane = lax.broadcasted_iota(jnp.int32, shape, 1)
    low = lane < 64
    phase = row % 4
    even = phase % 2 == 1
    sigma = jnp.where(even, 1.0, -1.0)
    kappa = jnp.where(
        phase == 1, -1.0, jnp.where(phase == 3, 1.0, jnp.where((phase == 0) == low, 1.0, -1.0))
    )
    for part in range(4):
        rows = slice(96 * part, 96 * part + 96)
        irows = slice(BINS + 96 * part, BINS + 96 * part + 96)
        a_sum = zs[rows, :128] + sigma * zs[rows, 128:]
        b_sum = zs[irows, :128] + sigma * zs[irows, 128:]
        a_roll = pltpu.roll(a_sum, 64, 1)
        b_roll = pltpu.roll(b_sum, 64, 1)
        first = jnp.where(low, a_sum, b_roll)
        other = jnp.where(
            even, jnp.where(low, a_roll, b_sum), jnp.where(low, b_roll, a_sum)
        )
        raw = first + kappa * other
        spec[rows, :] = raw
        square = raw * raw
        power = square + pltpu.roll(square, 64, 1)
        high = power.astype(jnp.bfloat16).astype(jnp.float32)
        n32[rows, :128] = jnp.where(low, high, power - high)

    frow = lax.broadcasted_iota(jnp.int32, (BINS, BINS), 0)
    gcol = lax.broadcasted_iota(jnp.int32, (BINS, BINS), 1)
    near = jnp.where(jnp.abs(frow - gcol) <= HALF, 1.0, 0.0).astype(jnp.bfloat16)
    total = jnp.dot(
        near, n32[:BINS, :128].astype(jnp.bfloat16), preferred_element_type=jnp.float32
    )
    frow = lax.broadcasted_iota(jnp.int32, (BINS, 128), 0)
    count = jnp.minimum(frow + HALF, BINS - 1) - jnp.maximum(frow - HALF, 0) + 1
    smooth = (total + pltpu.roll(total, 64, 1)) / count.astype(jnp.float32)
    spec[:BINS, :] = spec[:BINS, :] * lax.rsqrt(smooth + 1e-05)
    spec[BINS:, :] = jnp.zeros((8, 128), jnp.float32)
    for dev in range(NSEG):
        send[dev] = spec[pl.ds(PER * dev, ROWS), :].astype(jnp.bfloat16)


def kernel(
    xv, t_hbm, o_ref,
    tv, n32, x4, zs, spec, send, recv, r32, gath, wt,
    in_sem, a_send, a_recv, s_send, s_recv, g_send, g_recv,
):
    blk = lax.axis_index("blk")
    band = lax.axis_index("band")
    yy = blk // 2
    zz = lax.rem(blk, 2)
    hi = band // 2
    core = lax.rem(band, 2)
    partner = yy * 2 + 1 - zz
    near = [lax.rem(yy + dy + NY, NY) * 2 + z for dy in DY for z in (zz, 1 - zz)] + [partner]
    sibling = hi * 2 + 1 - core

    barrier = pltpu.get_barrier_semaphore()

    def greet(k, carry):
        pl.semaphore_signal(
            barrier,
            inc=1,
            device_id={"blk": blk, "band": lax.rem(band + k, NSEG)},
            device_id_type=MESH,
        )
        return carry

    t_copy = pltpu.make_async_copy(t_hbm.at[0], tv, in_sem)
    t_copy.start()
    for other in near:
        pl.semaphore_signal(
            barrier, inc=1, device_id={"blk": other, "band": band}, device_id_type=MESH
        )
    lax.fori_loop(1, NSEG, greet, 0)

    whiten(xv.at[0], tv, n32, x4, zs, spec, send, t_copy.wait)

    pl.semaphore_wait(barrier, len(near) + NSEG - 1)

    def scatter(m, carry):
        for c in (0, 1):
            to = lax.rem(hi + m, NHI) * 2 + c
            pltpu.make_async_remote_copy(
                src_ref=send.at[to],
                dst_ref=recv.at[core, m],
                send_sem=a_send,
                recv_sem=a_recv.at[core],
                device_id={"blk": blk, "band": to},
                device_id_type=MESH,
            ).start()
        return carry

    lax.fori_loop(1, NHI, scatter, 0)
    to_sibling = pltpu.make_async_remote_copy(
        src_ref=send.at[sibling],
        dst_ref=recv.at[core, 0],
        send_sem=s_send,
        recv_sem=s_recv,
        device_id={"blk": blk, "band": sibling},
        device_id_type=MESH,
    )
    to_sibling.start()
    recv[core, 0] = send[band]
    others = pl.ds(1, NHI - 1)

    def collect(c):
        pltpu.make_async_copy(recv.at[c, others], recv.at[c, others], a_recv.at[c]).wait()
        pl.when(core != c)(to_sibling.wait_recv)
        for m in range(NHI):
            r32[c, pl.ds(ROWS * m, ROWS), :] = recv[c, m].astype(jnp.float32)
        for f in range(PER):
            gath[0, 0, c, f] = r32[c, pl.ds(f, NHI, stride=ROWS), :].astype(jnp.bfloat16)

    plan = make_plan()
    copies = [entry[1] for entry in plan if entry[0] == "start"]

    def described(copy):
        plane, slot, c, part, dy, dz = copy
        k = copies.index(copy)
        rows = pl.ds(PER // PARTS * part, PER // PARTS)
        to = lax.rem(yy + dy + NY, NY) * 2 + (1 - zz if dz else zz)
        return pltpu.make_async_remote_copy(
            src_ref=gath.at[plane, slot, c, rows],
            dst_ref=gath.at[(plane + dz) % 2, (slot + dy) % NY, c, rows],
            send_sem=g_send.at[k],
            recv_sem=g_recv.at[k],
            device_id={"blk": to, "band": band},
            device_id_type=MESH,
        )

    def stack(slots, part):
        columns = [
            pl.ds(pl.multiple_of(lax.rem(yy + NY - slot, NY) * 128, 128), 128) for slot in slots
        ]

        def pair(slot, f):
            g0 = jnp.concatenate([gath[zz, slot, 0, f], gath[zz, slot, 1, f]], axis=0)
            g1 = jnp.concatenate([gath[1 - zz, slot, 0, f], gath[1 - zz, slot, 1, f]], axis=0)
            top = jnp.concatenate([g0[:, :64], g1[:, :64]], axis=1)
            bottom = jnp.concatenate([g0[:, 64:], g1[:, 64:]], axis=1)
            return jnp.concatenate([top, bottom], axis=0)

        for f in range(PER // PARTS * part, PER // PARTS * (part + 1)):
            both = jnp.concatenate([pair(slot, f) for slot in slots], axis=1)
            out = jnp.dot(wt[f], both, preferred_element_type=jnp.float32)
            out = out.astype(jnp.bfloat16)
            for k, where in enumerate(columns):
                lanes = slice(128 * k, 128 * k + 128)
                o_ref[0, f, :, where] = out[:64, lanes]
                o_ref[1, f, :, where] = out[64:, lanes]

    def turn_own():
        wlow = lax.broadcasted_iota(jnp.int32, (NSEG, 128), 1) < 64
        for f in range(PER):
            own = jnp.concatenate(
                [r32[c, pl.ds(f, NHI, stride=ROWS), :] for c in (0, 1)], axis=0
            ) * (1.0 / NSEG)
            turned = pltpu.roll(own, 64, 1)
            turned = jnp.where(wlow, turned, -turned)
            wt[f] = jnp.transpose(jnp.concatenate([own, turned], axis=0)).astype(jnp.bfloat16)

    collect(0)
    turned_yet = False
    for entry in plan:
        if entry[0] == "second":
            collect(1)
        elif entry[0] == "start":
            described(entry[1]).start()
        elif entry[0] == "wait":
            if not turned_yet:
                turn_own()
                turned_yet = True
            described(entry[1]).wait_recv()
        else:
            stack(*entry[1:])

    for copy in copies:
        described(copy).wait_send()
    to_sibling.wait_send()
    for half in (0, 1):
        rest = pl.ds(0, NHI - 1)
        pltpu.make_async_copy(send.at[rest], send.at[rest], a_send).wait()


def shards(waveforms):
    table = jnp.asarray(make_table())
    bf16, f32 = jnp.bfloat16, jnp.float32
    n_copies = sum(entry[0] == "start" for entry in make_plan())
    return pl.pallas_call(
        kernel,
        out_shape=jax.ShapeDtypeStruct((2, PER, 64, 1024), bf16),
        in_specs=[
            pl.BlockSpec(memory_space=pltpu.VMEM),
            pl.BlockSpec(memory_space=pl.ANY),
        ],
        out_specs=pl.BlockSpec(memory_space=pltpu.VMEM),
        scratch_shapes=[
            pltpu.VMEM((2 * BINS, QPAD), bf16),
            pltpu.VMEM((BINS, SPAD), f32),
            pltpu.VMEM((256, QPAD), bf16),
            pltpu.VMEM((2 * BINS, 256), f32),
            pltpu.VMEM((BINS + 8, 128), f32),
            pltpu.VMEM((NSEG, ROWS, 128), bf16),
            pltpu.VMEM((2, NHI, ROWS, 128), bf16),
            pltpu.VMEM((2, NHI * ROWS, 128), f32),
            pltpu.VMEM((2, NY, 2, PER, NHI, 128), bf16),
            pltpu.VMEM((PER, 128, 64), bf16),
            pltpu.SemaphoreType.DMA,
            pltpu.SemaphoreType.DMA,
            pltpu.SemaphoreType.DMA((2,)),
            pltpu.SemaphoreType.DMA,
            pltpu.SemaphoreType.DMA,
            pltpu.SemaphoreType.DMA((n_copies,)),
            pltpu.SemaphoreType.DMA((n_copies,)),
        ],
        compiler_params=pltpu.CompilerParams(
            collective_id=0, has_side_effects=True, vmem_limit_bytes=44 * 1024 * 1024
        ),
        cost_estimate=pl.CostEstimate(
            flops=600_000_000, bytes_accessed=6_000_000, transcendentals=50_000
        ),
    )(waveforms, table)


def solution(mesh):
    return jax.shard_map(
        shards,
        mesh=mesh,
        in_specs=(P("band", "blk", None),),
        out_specs=P(None, "band", "blk", None),
        check_vma=False,
    )
```

```python
import heapq
import math

import jax
import jax.numpy as jnp
import numpy as np
import ml_dtypes
from jax import lax
from jax.experimental import pallas as pl
from jax.experimental.pallas import tpu as pltpu
from jax.sharding import PartitionSpec as P

L = 3000
BINS = 384
HALF = 64
QUARTER = 750
QPAD = 768
SPAD = 3072
PER = 12
ROWS = 16
NSEG = 32
NY = 8
MESH = pl.DeviceIdType.MESH
NHI = 16
TABLES = 16


def make_table():
    freqs = np.arange(1, BINS + 1, dtype=np.int64)
    samples = np.arange(QUARTER, dtype=np.int64)
    phase = ((freqs[:, None] * samples[None, :]) % L).astype(np.float64) * (2.0 * math.pi / L)
    table = np.zeros((TABLES, 2 * BINS, QPAD), ml_dtypes.bfloat16)
    table[0, :BINS, :QUARTER] = np.cos(phase).astype(np.float32).astype(ml_dtypes.bfloat16)
    table[0, BINS:, :QUARTER] = (-np.sin(phase)).astype(np.float32).astype(ml_dtypes.bfloat16)
    return table


PARTS = 3
PIECES = [(group, p) for group in (0, 1) for p in range(PARTS)]
Y_FIRST = PIECES[:4]
DIAGONAL = True
SKIP = True
DY = (1, -1, 2, -2)
LATENCY, HOP, LATE = 3.2, 0.55, 3.0
ORDER = (1, 0, 2, 3)
TURN = 0.8
GAP, WORK, BACKLOG = 0.1, 0.22, 0


def make_plan():
    unit, cost = 1.07 / PARTS, 0.06
    last = {}
    for plane in (0, 1):
        for piece in PIECES:
            if plane == 0 or piece not in Y_FIRST:
                last[plane, *piece] = (1, -1)[len(last) % 2]
    free = {1: 0.0, -1: 0.0, 0: 0.0}
    arrivals, plan = [], []
    now = 0.0

    def start(plane, slot, piece, dy, dz):
        nonlocal now
        now += cost
        sign = (dy > 0) - (dy < 0)
        links = ([sign] if dy else []) + ([0] if dz else [])
        first = max([free[k] for k in links] + [now])
        for k in links:
            free[k] = max(free[k], first) + unit * (abs(dy) if k else 1)
        copy = (plane, slot, *piece, dy, dz)
        arrival = first + unit + LATENCY + HOP * (abs(dy) + dz - 1)
        heapq.heappush(arrivals, (arrival, len(plan), copy))
        plan.append(("start", copy))

    def begin(group):
        mine = [piece for piece in PIECES if piece[0] == group]
        for piece in mine:
            if piece not in Y_FIRST:
                start(0, 0, piece, 0, 1)
        for piece in mine:
            for sign in (1, -1):
                start(0, 0, piece, sign, 0)
            if piece not in Y_FIRST and DIAGONAL:
                for sign in (1, -1):
                    start(0, 0, piece, sign, 1)
        for piece in mine:
            if piece in Y_FIRST:
                start(0, 0, piece, 0, 1)

    begin(0)
    heapq.heappush(arrivals, (LATE, -1, None))
    missing = {(slot, p): 4 if slot else 2 for slot in range(NY) for p in range(PARTS)}
    groups = [(0,), (1, 7), (2, 6), (3, 5), (4,)]
    ready = []
    while arrivals:
        while ready and arrivals[0][0] - now > GAP:
            plan.append(ready.pop(0))
            now += WORK
        when, _, copy = heapq.heappop(arrivals)
        now = max(now, when) + cost
        if copy is None:
            plan.append(("second",))
            begin(1)
            plan.append(("turn",))
            now += TURN
            continue
        plan.append(("wait", copy))
        plane, slot, core, part, dy, dz = copy
        piece = (core, part)
        plane, slot = (plane + dz) % 2, (slot + dy) % NY
        sign = (dy > 0) - (dy < 0)
        first_cross = plane == 1 and piece not in Y_FIRST
        if dy == 0:
            if slot == 0 and first_cross and not DIAGONAL:
                for sign in (1, -1):
                    start(1, 0, piece, sign, 0)
        elif plane == 0 or first_cross:
            distance = min(slot, NY - slot)
            if distance < 3:
                start(plane, slot, piece, sign, 0)
            if last[plane, core, part] == sign and distance == (2 if SKIP else 3):
                start(plane, slot, piece, (2 if SKIP else 1) * sign, 0)
            if plane == 0 and piece in Y_FIRST:
                start(0, slot, piece, 0, 1)
        missing[slot, part] -= 1
        for group in groups:
            if slot in group and not any(missing[k, part] for k in group):
                ready.append(("stack", group, part))
        if len(ready) > BACKLOG:
            plan.append(ready.pop(0))
            now += WORK
    plan.extend(ready)
    assert not any(missing.values())
    return plan


def whiten(xv, tv, n32, x4, zs, spec, send, table_ready):
    for block in range(4):
        rows = pl.ds(16 * block, 16)
        values = xv[rows, :].astype(jnp.float32)
        centred = values - jnp.sum(values, axis=1, keepdims=True) * (1.0 / L)
        var = jnp.sum(centred * centred, axis=1, keepdims=True) * (1.0 / L)
        n32[rows, SPAD - 128 :] = jnp.zeros((16, 128), jnp.float32)
        n32[rows, :L] = centred * lax.rsqrt(var + 1e-05)
        x4[rows, :] = n32[rows, :QPAD].astype(jnp.bfloat16)
        for q in range(1, 4):
            start = QUARTER * q // 128 * 128
            off = QUARTER * q - start
            window = n32[rows, start : start + 896]
            window = pltpu.roll(window, 896 - off, 1)
            x4[pl.ds(64 * q + 16 * block, 16), :] = window[:, :QPAD].astype(jnp.bfloat16)

    table_ready()
    zs[...] = lax.dot_general(
        tv[...], x4[...], (((1,), (1,)), ((), ())), preferred_element_type=jnp.float32
    )

    shape = (96, 128)
    row = lax.broadcasted_iota(jnp.int32, shape, 0)
    lane = lax.broadcasted_iota(jnp.int32, shape, 1)
    low = lane < 64
    phase = row % 4
    even = phase % 2 == 1
    sigma = jnp.where(even, 1.0, -1.0)
    kappa = jnp.where(
        phase == 1, -1.0, jnp.where(phase == 3, 1.0, jnp.where((phase == 0) == low, 1.0, -1.0))
    )
    for part in range(4):
        rows = slice(96 * part, 96 * part + 96)
        irows = slice(BINS + 96 * part, BINS + 96 * part + 96)
        a_sum = zs[rows, :128] + sigma * zs[rows, 128:]
        b_sum = zs[irows, :128] + sigma * zs[irows, 128:]
        a_roll = pltpu.roll(a_sum, 64, 1)
        b_roll = pltpu.roll(b_sum, 64, 1)
        first = jnp.where(low, a_sum, b_roll)
        other = jnp.where(
            even, jnp.where(low, a_roll, b_sum), jnp.where(low, b_roll, a_sum)
        )
        raw = first + kappa * other
        spec[rows, :] = raw
        square = raw * raw
        power = square + pltpu.roll(square, 64, 1)
        high = power.astype(jnp.bfloat16).astype(jnp.float32)
        n32[rows, :128] = jnp.where(low, high, power - high)

    frow = lax.broadcasted_iota(jnp.int32, (BINS, BINS), 0)
    gcol = lax.broadcasted_iota(jnp.int32, (BINS, BINS), 1)
    near = jnp.where(jnp.abs(frow - gcol) <= HALF, 1.0, 0.0).astype(jnp.bfloat16)
    total = jnp.dot(
        near, n32[:BINS, :128].astype(jnp.bfloat16), preferred_element_type=jnp.float32
    )
    frow = lax.broadcasted_iota(jnp.int32, (BINS, 128), 0)
    count = jnp.minimum(frow + HALF, BINS - 1) - jnp.maximum(frow - HALF, 0) + 1
    smooth = (total + pltpu.roll(total, 64, 1)) / count.astype(jnp.float32)
    spec[:BINS, :] = spec[:BINS, :] * lax.rsqrt(smooth + 1e-05)
    spec[BINS:, :] = jnp.zeros((8, 128), jnp.float32)
    for dev in range(NSEG):
        send[dev] = spec[pl.ds(PER * dev, ROWS), :].astype(jnp.bfloat16)


def kernel(
    xv, t_hbm, o_ref,
    tv, n32, x4, zs, spec, send, recv, r32, gath, wt,
    in_sem, a_send, a_recv, s_send, s_recv, g_send, g_recv,
):
    blk = lax.axis_index("blk")
    band = lax.axis_index("band")
    yy = blk // 2
    zz = lax.rem(blk, 2)
    xx = band // 8
    zhi = lax.rem(band // 2, 4)
    core = lax.rem(band, 2)
    partner = yy * 2 + 1 - zz
    near = [lax.rem(yy + dy + NY, NY) * 2 + z for dy in DY for z in (zz, 1 - zz)] + [partner]
    sibling = band + 1 - 2 * core

    barrier = pltpu.get_barrier_semaphore()

    t_copy = pltpu.make_async_copy(t_hbm.at[0], tv, in_sem)
    t_copy.start()
    for dz in (0, 1, 3, 2):
        for dx in (2, 1, 3, 0):
            for c in (0, 1) if dx or dz else ():
                to = lax.rem(xx + dx, 4) * 8 + lax.rem(zhi + dz, 4) * 2 + c
                pl.semaphore_signal(
                    barrier, inc=1, device_id={"blk": blk, "band": to}, device_id_type=MESH
                )
    for other in near:
        pl.semaphore_signal(
            barrier, inc=1, device_id={"blk": other, "band": band}, device_id_type=MESH
        )
    pl.semaphore_signal(
        barrier, inc=1, device_id={"blk": blk, "band": sibling}, device_id_type=MESH
    )

    whiten(xv.at[0], tv, n32, x4, zs, spec, send, t_copy.wait)

    pl.semaphore_wait(barrier, len(near) + NSEG - 1)

    def send_to(dx, dz):
        chip = lax.rem(xx + dx, 4) * 8 + lax.rem(zhi + dz, 4) * 2
        for c in (0, 1):
            pltpu.make_async_remote_copy(
                src_ref=send.at[chip + c],
                dst_ref=recv.at[dz // 2, 4 * dx + 2 * (dz % 2) + core],
                send_sem=a_send,
                recv_sem=a_recv.at[dz // 2],
                device_id={"blk": blk, "band": chip + c},
                device_id_type=MESH,
            ).start()

    for dz in ORDER:
        for dx in (2, 1, 3, 0):
            if dx or dz:
                send_to(dx, dz)
    to_sibling = pltpu.make_async_remote_copy(
        src_ref=send.at[sibling],
        dst_ref=recv.at[0, core],
        send_sem=s_send,
        recv_sem=s_recv,
        device_id={"blk": blk, "band": sibling},
        device_id_type=MESH,
    )
    to_sibling.start()
    recv[0, core] = send[band]

    def collect(group):
        came = pl.ds(0, NHI) if group else pl.ds(2, NHI - 2)
        pltpu.make_async_copy(recv.at[group, came], recv.at[group, came], a_recv.at[group]).wait()
        if group == 0:
            to_sibling.wait_recv()
        for k in range(NHI):
            r32[group, pl.ds(ROWS * k, ROWS), :] = recv[group, k].astype(jnp.float32)
        for f in range(PER):
            gath[0, 0, group, f] = r32[group, pl.ds(f, NHI, stride=ROWS), :].astype(jnp.bfloat16)

    plan = make_plan()
    copies = [entry[1] for entry in plan if entry[0] == "start"]

    def described(copy):
        plane, slot, c, part, dy, dz = copy
        k = copies.index(copy)
        rows = pl.ds(PER // PARTS * part, PER // PARTS)
        to = lax.rem(yy + dy + NY, NY) * 2 + (1 - zz if dz else zz)
        return pltpu.make_async_remote_copy(
            src_ref=gath.at[plane, slot, c, rows],
            dst_ref=gath.at[(plane + dz) % 2, (slot + dy) % NY, c, rows],
            send_sem=g_send,
            recv_sem=g_recv.at[k],
            device_id={"blk": to, "band": band},
            device_id_type=MESH,
        )

    def stack(slots, part):
        columns = [
            pl.ds(pl.multiple_of(lax.rem(yy + NY - slot, NY) * 128, 128), 128) for slot in slots
        ]

        def pair(slot, f):
            g0 = jnp.concatenate([gath[zz, slot, 0, f], gath[zz, slot, 1, f]], axis=0)
            g1 = jnp.concatenate([gath[1 - zz, slot, 0, f], gath[1 - zz, slot, 1, f]], axis=0)
            top = jnp.concatenate([g0[:, :64], g1[:, :64]], axis=1)
            bottom = jnp.concatenate([g0[:, 64:], g1[:, 64:]], axis=1)
            return jnp.concatenate([top, bottom], axis=0)

        for f in range(PER // PARTS * part, PER // PARTS * (part + 1)):
            both = jnp.concatenate([pair(slot, f) for slot in slots], axis=1)
            out = jnp.dot(wt[f], both, preferred_element_type=jnp.float32)
            out = out.astype(jnp.bfloat16)
            for k, where in enumerate(columns):
                lanes = slice(128 * k, 128 * k + 128)
                o_ref[0, f, :, where] = out[:64, lanes]
                o_ref[1, f, :, where] = out[64:, lanes]

    def turn_own():
        wlow = lax.broadcasted_iota(jnp.int32, (NSEG, 128), 1) < 64
        for f in range(PER):
            own = jnp.concatenate(
                [r32[c, pl.ds(f, NHI, stride=ROWS), :] for c in (0, 1)], axis=0
            ) * (1.0 / NSEG)
            turned = pltpu.roll(own, 64, 1)
            turned = jnp.where(wlow, turned, -turned)
            wt[f] = jnp.transpose(jnp.concatenate([own, turned], axis=0)).astype(jnp.bfloat16)

    collect(0)
    for entry in plan:
        if entry[0] == "second":
            collect(1)
        elif entry[0] == "turn":
            turn_own()
        elif entry[0] == "start":
            described(entry[1]).start()
        elif entry[0] == "wait":
            described(entry[1]).wait_recv()
        else:
            stack(*entry[1:])

    whole = 4 * NY * PARTS
    for _ in range(len(copies) // whole):
        pltpu.make_async_copy(gath, gath, g_send).wait()
    size = PER // PARTS
    spare = len(copies) % whole
    for piece in range(spare):
        one = gath.at[0, 0, 0, pl.ds(0, size)]
        pltpu.make_async_copy(one, one, g_send).wait()
    to_sibling.wait_send()
    for half in (0, 1):
        rest = pl.ds(0, NHI - 1)
        pltpu.make_async_copy(send.at[rest], send.at[rest], a_send).wait()


def shards(waveforms):
    table = jnp.asarray(make_table())
    bf16, f32 = jnp.bfloat16, jnp.float32
    n_copies = sum(entry[0] == "start" for entry in make_plan())
    return pl.pallas_call(
        kernel,
        out_shape=jax.ShapeDtypeStruct((2, PER, 64, 1024), bf16),
        in_specs=[
            pl.BlockSpec(memory_space=pltpu.VMEM),
            pl.BlockSpec(memory_space=pl.ANY),
        ],
        out_specs=pl.BlockSpec(memory_space=pltpu.VMEM),
        scratch_shapes=[
            pltpu.VMEM((2 * BINS, QPAD), bf16),
            pltpu.VMEM((BINS, SPAD), f32),
            pltpu.VMEM((256, QPAD), bf16),
            pltpu.VMEM((2 * BINS, 256), f32),
            pltpu.VMEM((BINS + 8, 128), f32),
            pltpu.VMEM((NSEG, ROWS, 128), bf16),
            pltpu.VMEM((2, NHI, ROWS, 128), bf16),
            pltpu.VMEM((2, NHI * ROWS, 128), f32),
            pltpu.VMEM((2, NY, 2, PER, NHI, 128), bf16),
            pltpu.VMEM((PER, 128, 64), bf16),
            pltpu.SemaphoreType.DMA,
            pltpu.SemaphoreType.DMA,
            pltpu.SemaphoreType.DMA((2,)),
            pltpu.SemaphoreType.DMA,
            pltpu.SemaphoreType.DMA,
            pltpu.SemaphoreType.DMA,
            pltpu.SemaphoreType.DMA((n_copies,)),
        ],
        compiler_params=pltpu.CompilerParams(
            collective_id=0, has_side_effects=True, vmem_limit_bytes=44 * 1024 * 1024
        ),
        cost_estimate=pl.CostEstimate(
            flops=600_000_000, bytes_accessed=6_000_000, transcendentals=50_000
        ),
    )(waveforms, table)


def solution(mesh):
    return jax.shard_map(
        shards,
        mesh=mesh,
        in_specs=(P("band", "blk", None),),
        out_specs=P(None, "band", "blk", None),
        check_vma=False,
    )
```
